32 devices in a mesh: morton: 16 (over z, y, x), sub: 2 (over core).
Axes of the slice: x: 2, y: 2, z: 4, core: 2. Of those that a mesh axis runs over, the one named last changes fastest.
Arguments:
- fine_multipole: bfloat16 [64, 32768], P(None, 'morton'), may hold values from -6 to 6
- coarse_multipole: bfloat16 [64, 5120], P(None, ('morton', 'sub')), may hold values from -6 to 6
- kernels: bfloat16 [316, 64, 64], P('sub'), may hold values from -0.0625 to 0.0625
- send_list: int32 [16, 16, 384], P('morton'), may hold values from 0 to 2047
- fine_source: int32 [316, 32768], P('sub', 'morton'), may hold values from 0 to 8192, as said below
- coarse_source: int32 [316, 5120], P('sub', 'morton'), may hold values from 0 to 5120, as said below
Outputs:
- fine_local: float32 [64, 32768], P(None, ('morton', 'sub'))
- coarse_local: float32 [64, 5120], P(None, ('morton', 'sub'))
The draws below stay inside these ranges and needn't reach their ends.
Inputs may be any that keep to these rules, and one draw needn't show every extreme that they name: `fine_source`: values below 2048 name a box of the target's own Morton range m; the value 2048 + j * 384 + k names slot k of what range m + d_j sends to m, and that range always lies in 0 to 15; the value 2048 + 2 * 8 * 384 means no interaction. `coarse_source`: A value below 5120 names an upper-level source box; the value 5120 means no interaction.
All inputs are finite; a program needn't handle non-finite values.
Results may differ from the reference program's by a relative error of at most 0.0003.
Values may be sent and summed in bfloat16 or wider, within the bound.
A program may use at most 128 MiB of HBM per device.

```python
import math
import jax
import jax.numpy as jnp
from jax import lax

P_SIZE = 64
OFFSETS = 316
REACH = 8
BOX_DEV = 2048
COARSE_DEV = 320
GHOST = 384
BOXES = 32768
COARSE = 5120
N_MORTON = 16


def draw_fine_source(key, part):
    key = jax.random.fold_in(key, 11)
    subkeys = jax.random.split(key, 7)
    boxes = BOX_DEV * N_MORTON
    shape = (OFFSETS, boxes)
    owner = (jnp.arange(boxes, dtype=jnp.int32) // BOX_DEV)[None, :]
    levels = jax.random.randint(subkeys[0], (N_MORTON,), 10, 70)
    absent_level = jnp.take(levels, owner)
    chance = jax.random.randint(subkeys[1], shape, 0, 100)
    local_box = jax.random.randint(subkeys[2], shape, 0, BOX_DEV)
    ladder = jax.random.randint(subkeys[3], shape, 0, 8)
    tail_step = jax.random.randint(subkeys[4], shape, 1, REACH + 1)
    distance = jnp.where(ladder < 4, 1, jnp.where(ladder < 6, 2, jnp.where(ladder < 7, 3, tail_step)))
    distance = jnp.minimum(distance, REACH)
    upward = jax.random.randint(subkeys[5], shape, 0, 2)
    signed = jnp.where(upward == 1, distance, -distance)
    landing = owner + signed
    signed = jnp.where((landing < 0) | (landing >= N_MORTON), -signed, signed)
    column = jnp.where(signed < 0, signed + REACH, signed + REACH - 1)
    slot_pick = jax.random.randint(subkeys[6], shape, 0, GHOST)
    ghost_value = BOX_DEV + column * GHOST + slot_pick
    missing = BOX_DEV + 2 * REACH * GHOST
    local_limit = absent_level + (100 - absent_level) * 3 // 4
    value = jnp.where(chance < absent_level, missing, jnp.where(chance < local_limit, local_box, ghost_value))
    return value.astype(jnp.int32)


def draw_coarse_source(key, part):
    key = jax.random.fold_in(key, 23)
    subkeys = jax.random.split(key, 3)
    total = COARSE_DEV * N_MORTON
    shape = (OFFSETS, total)
    owner = (jnp.arange(total, dtype=jnp.int32) // COARSE_DEV)[None, :]
    levels = jax.random.randint(subkeys[0], (N_MORTON,), 10, 70)
    absent_level = jnp.take(levels, owner)
    chance = jax.random.randint(subkeys[1], shape, 0, 100)
    chosen = jax.random.randint(subkeys[2], shape, 0, total)
    return jnp.where(chance < absent_level, total, chosen).astype(jnp.int32)


def set_ends(drawn, stream_key, low, largest):
    longest = drawn.shape.index(max(drawn.shape))
    spots = []
    for shift in (0, 1):
        where = [jax.random.randint(jax.random.fold_in(stream_key, axis), (), 0, length) for axis, length in enumerate(drawn.shape)]
        where[longest] = (where[longest] + shift) % drawn.shape[longest]
        spots.append(tuple(where))
    return drawn.at[spots[0]].set(low).at[spots[1]].set(largest)


def block_scale(rng, dims, shards, least, largest):
    def one(position, parts):
        heights = jax.random.uniform(jax.random.fold_in(jax.random.fold_in(rng, 6), position), (parts,), jnp.float32, least / len(shards), largest / len(shards))
        return jnp.repeat(jnp.exp(heights), dims[position] // parts).reshape((-1,) + (1,) * (len(dims) - position - 1))

    level = one(*shards[0])
    for cut in shards[1:]:
        level = level * one(*cut)
    return level


def gaussian(rng, extent, spread, most, cuts=(), held_as=jnp.bfloat16):
    loudness = block_scale(rng, extent, cuts, -0.22, 0.18) if cuts else 1.0
    array = jax.random.normal(rng, extent, jnp.float32) * spread * loudness
    return jnp.minimum(jnp.maximum(array, -most), most).astype(held_as)


def setup_inputs(seed: int = 0) -> dict:
    key_of = jax.random.split(jax.random.key(seed), 7)
    return {
        "fine_multipole": gaussian(key_of[0], (P_SIZE, BOXES), 1.0, 6.0, ((1, 16),)),
        "coarse_multipole": gaussian(key_of[1], (P_SIZE, COARSE), 1.0, 6.0, ((1, 32),)),
        "kernels": gaussian(key_of[2], (OFFSETS, P_SIZE, P_SIZE), (P_SIZE * OFFSETS // 2) ** -0.5, 0.0625, ((0, 2),)),
        "send_list": set_ends(jax.random.randint(key_of[3], (N_MORTON, 2 * REACH, GHOST), 0, BOX_DEV), jax.random.fold_in(key_of[3], 1), 0, BOX_DEV - 1).astype(jnp.int32),
        "fine_source": draw_fine_source(jax.random.fold_in(key_of[6], 71), 0),
        "coarse_source": draw_coarse_source(jax.random.fold_in(key_of[6], 71), 0),
    }


def translate(tables, columns, lists, block):
    number = lists.shape[1] // block

    def one_block(index):
        chosen = lax.dynamic_slice_in_dim(lists, index * block, block, 1)
        gathered = jnp.take(columns, chosen, axis=1)
        return jnp.einsum("opq,qob->pb", tables, gathered, precision=lax.Precision.HIGHEST)

    blocks = lax.map(one_block, jnp.arange(number, dtype=jnp.int32))
    return jnp.transpose(blocks, (1, 0, 2)).reshape(tables.shape[1], lists.shape[1])


def reference(fine_multipole, coarse_multipole, kernels, send_list, fine_source, coarse_source):
    tables = kernels.astype(jnp.float32)
    width = fine_multipole.shape[0]
    fine_cols = jnp.concatenate([fine_multipole.astype(jnp.float32), jnp.zeros((width, 1), jnp.float32)], axis=1)
    coarse_cols = jnp.concatenate([coarse_multipole.astype(jnp.float32), jnp.zeros((width, 1), jnp.float32)], axis=1)
    flat_send = send_list.reshape(-1)
    owner = (jnp.arange(BOXES, dtype=jnp.int32) // BOX_DEV)[None, :]
    relative = fine_source - BOX_DEV
    column = jnp.clip(relative // GHOST, 0, 2 * REACH - 1)
    slot_index = relative % GHOST
    distance = jnp.where(column < REACH, column - REACH, column - REACH + 1)
    source_range = jnp.clip(owner + distance, 0, N_MORTON - 1)
    remote = source_range * BOX_DEV + jnp.take(flat_send, (source_range * (2 * REACH) + column) * GHOST + slot_index)
    own_box = owner * BOX_DEV + fine_source
    source = jnp.where(fine_source < BOX_DEV, own_box, jnp.where(fine_source < BOX_DEV + 2 * REACH * GHOST, remote, BOXES)).astype(jnp.int32)
    fine_local = translate(tables, fine_cols, source, math.gcd(BOXES, 512))
    coarse_local = 0.5 * translate(tables, coarse_cols, coarse_source, math.gcd(COARSE, 512))
    return fine_local, coarse_local
```

```python
import functools
import math

import jax
import jax.numpy as jnp
from jax import lax
from jax.experimental import pallas as pl
from jax.experimental.pallas import tpu as pltpu
from jax.sharding import PartitionSpec as P

GROUP = 4
BATCH = 8
BLANK = 16


def passed_along(block, axis, distance):
    devices = range(lax.axis_size(axis))
    route = [(i - distance, i) for i in devices if i - distance in devices]
    return lax.ppermute(block, axis, route)


def gather_multiply(targets, chunk, steps, offset_ref, index_ref, table_ref, kernel_ref, out_ref, held_ref):
    step = pl.program_id(0)
    width = out_ref.shape[1]

    @pl.when(step == 0)
    def _():
        out_ref[...] = jnp.zeros_like(out_ref)
        held_ref[...] = jnp.zeros_like(held_ref)

    left = lax.broadcasted_iota(jnp.int32, (1, 2 * width), 1) < width

    offsets = [offset_ref[t] for t in range(BATCH)]

    def product(rows):
        lhs = jnp.concatenate([held_ref[pair, rows, :] for pair in range(GROUP // 2)], axis=1)
        return jnp.dot(
            lhs.astype(jnp.bfloat16), kernel_ref[0], preferred_element_type=jnp.float32
        )

    def fetch(indices, batch):
        rows = []
        for pair in range(GROUP // 2):
            for t in range(BATCH):
                spot = 2 * pair * chunk + batch * BATCH
                first = table_ref[indices.at[pl.ds(spot, BATCH)][offsets[t]]]
                second = table_ref[indices.at[pl.ds(spot + chunk, BATCH)][offsets[t]]]
                rows.append(jnp.where(left, first, second))
        return rows

    def keep(base, batch, rows):
        for pair in range(GROUP // 2):
            for t in range(BATCH):
                held_ref[pair, pl.ds(base + (batch * BATCH + t), 1), :] = rows[pair * BATCH + t]

    @pl.when(step < steps)
    def _():
        @pl.loop(0, targets // chunk)
        def _(c):
            base = pl.multiple_of(c * chunk, chunk)
            rows = pl.ds(base, chunk)
            done = product(rows)
            indices = index_ref.at[0, c, 0]
            pending = fetch(indices, 0)
            for batch in range(1, chunk // BATCH):
                coming = fetch(indices, batch)
                keep(base, batch - 1, pending)
                pending = coming
            keep(base, chunk // BATCH - 1, pending)
            out_ref[rows, :] += done

    @pl.when(step == steps)
    def _():
        @pl.loop(0, targets // chunk)
        def _(c):
            rows = pl.ds(pl.multiple_of(c * chunk, chunk), chunk)
            out_ref[rows, :] += product(rows)


def translate(tables, table, lists):
    offsets, width, _ = tables.shape
    targets = lists.shape[1]
    chunk = math.gcd(targets, 64)
    steps = -(-offsets // GROUP)
    weights = jnp.transpose(tables, (0, 2, 1))
    weights = jnp.pad(weights, ((0, steps * GROUP - offsets), (0, 0), (0, 0)))
    weights = weights.reshape(steps, GROUP * width, width)
    parts = targets // chunk
    index = jnp.transpose(lists.reshape(steps, GROUP, parts, chunk), (0, 2, 1, 3))
    index = index.reshape(steps, parts, 1, GROUP * chunk)
    return pl.pallas_call(
        functools.partial(gather_multiply, targets, chunk, steps),
        grid=(steps + 1,),
        out_shape=jax.ShapeDtypeStruct((targets, width), jnp.float32),
        in_specs=[
            pl.BlockSpec(memory_space=pltpu.SMEM),
            pl.BlockSpec(
                (1, parts, 1, GROUP * chunk),
                lambda i: (jnp.minimum(i, steps - 1), 0, 0, 0),
                memory_space=pltpu.SMEM,
            ),
            pl.BlockSpec(
                table.shape, lambda i: (0, 0, 0), pipeline_mode=pl.Buffered(1)
            ),
            pl.BlockSpec(
                (1, GROUP * width, width), lambda i: (jnp.maximum(i - 1, 0), 0, 0)
            ),
        ],
        out_specs=pl.BlockSpec((targets, width), lambda i: (0, 0)),
        scratch_shapes=[pltpu.VMEM((GROUP // 2, targets, 2 * width), jnp.float32)],
        compiler_params=pltpu.CompilerParams(
            vmem_limit_bytes=48 * 1024 * 1024, dimension_semantics=("arbitrary",)
        ),
    )(jnp.arange(BATCH, dtype=jnp.int32), index, table, weights)


def per_device(fine_multipole, coarse_multipole, kernels, send_list, fine_source, coarse_source):
    width = fine_multipole.shape[0]
    reach_each = send_list.shape[1] // 2
    ghost_slots = send_list.shape[2]
    near_steps = [
        j - reach_each if j < reach_each else j - reach_each + 1 for j in range(2 * reach_each)
    ]
    own = jnp.transpose(fine_multipole)
    outgoing = jnp.take(own, send_list[0].reshape(-1), axis=0, mode="clip").reshape(
        2 * reach_each, ghost_slots, width
    )
    arrivals = [
        passed_along(outgoing[j], "morton", -near_steps[j]) for j in range(2 * reach_each)
    ]
    coarse = lax.all_gather(
        jnp.transpose(coarse_multipole), ("morton", "sub"), axis=0, tiled=True
    )
    blank = jnp.zeros((BLANK, width), jnp.bfloat16)
    rows = jnp.concatenate([own, *arrivals, blank, coarse, blank], axis=0)
    rows = rows.astype(jnp.float32)
    table = jnp.concatenate([rows, rows], axis=1)[:, None, :]
    no_source = own.shape[0] + 2 * reach_each * ghost_slots
    fine_half = fine_source.shape[1] // 2
    coarse_half = coarse_source.shape[1] // 2
    coarse_index = coarse_source + (no_source + BLANK)
    lists = jnp.concatenate(
        [
            fine_source[:, :fine_half],
            coarse_index[:, :coarse_half],
            fine_source[:, fine_half:],
            coarse_index[:, coarse_half:],
        ],
        axis=1,
    )
    extra = -lists.shape[0] % GROUP
    lists = jnp.pad(lists, ((0, extra), (0, 0)), constant_values=no_source)
    part = translate(kernels, table, lists)
    local = lax.psum_scatter(part, "sub", scatter_dimension=0, tiled=True)
    local = jnp.transpose(local)
    return local[:, :fine_half], 0.5 * local[:, fine_half:]


def solution(mesh):
    placed = (
        P(None, "morton"),
        P(None, ("morton", "sub")),
        P("sub", None, None),
        P("morton", None, None),
        P("sub", "morton"),
        P("sub", "morton"),
    )
    return jax.shard_map(
        per_device,
        mesh=mesh,
        in_specs=placed,
        out_specs=(P(None, ("morton", "sub")), P(None, ("morton", "sub"))),
        check_vma=False,
    )
```

```python
import functools
import math

import jax
import jax.numpy as jnp
from jax import lax
from jax.experimental import pallas as pl
from jax.experimental.pallas import tpu as pltpu
from jax.sharding import PartitionSpec as P

GROUP = 4
BATCH = 8
BLANK = 16


def side_by_side(blocks):
    half = blocks.shape[1] // 2
    return jnp.concatenate([blocks[:, :half], blocks[:, half:]], axis=2)


def one_below_other(blocks):
    half = blocks.shape[2] // 2
    return jnp.concatenate([blocks[:, :, :half], blocks[:, :, half:]], axis=1)


def gather_multiply(targets, chunk, steps, offset_ref, index_ref, table_ref, kernel_ref, out_ref, held_ref):
    step = pl.program_id(0)
    width = out_ref.shape[1]

    @pl.when(step == 0)
    def _():
        out_ref[...] = jnp.zeros_like(out_ref)
        held_ref[...] = jnp.zeros_like(held_ref)

    left = lax.broadcasted_iota(jnp.int32, (1, 2 * width), 1) < width

    offsets = [offset_ref[t] for t in range(BATCH)]

    def product(rows):
        lhs = jnp.concatenate([held_ref[pair, rows, :] for pair in range(GROUP // 2)], axis=1)
        return jnp.dot(
            lhs.astype(jnp.bfloat16), kernel_ref[0], preferred_element_type=jnp.float32
        )

    def fetch(indices, batch):
        rows = []
        for pair in range(GROUP // 2):
            for t in range(BATCH):
                spot = 2 * pair * chunk + batch * BATCH
                first = table_ref[indices.at[pl.ds(spot, BATCH)][offsets[t]]]
                second = table_ref[indices.at[pl.ds(spot + chunk, BATCH)][offsets[t]]]
                rows.append(jnp.where(left, first, second))
        return rows

    def keep(base, batch, rows):
        for pair in range(GROUP // 2):
            for t in range(BATCH):
                held_ref[pair, pl.ds(base + (batch * BATCH + t), 1), :] = rows[pair * BATCH + t]

    @pl.when(step < steps)
    def _():
        @pl.loop(0, targets // chunk)
        def _(c):
            base = pl.multiple_of(c * chunk, chunk)
            rows = pl.ds(base, chunk)
            done = product(rows)
            indices = index_ref.at[0, c, 0]
            pending = fetch(indices, 0)
            for batch in range(1, chunk // BATCH):
                coming = fetch(indices, batch)
                keep(base, batch - 1, pending)
                pending = coming
            keep(base, chunk // BATCH - 1, pending)
            out_ref[rows, :] += done

    @pl.when(step == steps)
    def _():
        @pl.loop(0, targets // chunk)
        def _(c):
            rows = pl.ds(pl.multiple_of(c * chunk, chunk), chunk)
            out_ref[rows, :] += product(rows)


def translate(tables, table, lists):
    offsets, width, _ = tables.shape
    targets = lists.shape[1]
    chunk = math.gcd(targets, 64)
    steps = -(-offsets // GROUP)
    weights = jnp.transpose(tables, (0, 2, 1))
    weights = jnp.pad(weights, ((0, steps * GROUP - offsets), (0, 0), (0, 0)))
    weights = weights.reshape(steps, GROUP * width, width)
    parts = targets // chunk
    index = jnp.transpose(lists.reshape(steps, GROUP, parts, chunk), (0, 2, 1, 3))
    index = index.reshape(steps, parts, 1, GROUP * chunk)
    return pl.pallas_call(
        functools.partial(gather_multiply, targets, chunk, steps),
        grid=(steps + 1,),
        out_shape=jax.ShapeDtypeStruct((targets, width), jnp.float32),
        in_specs=[
            pl.BlockSpec(memory_space=pltpu.SMEM),
            pl.BlockSpec(
                (1, parts, 1, GROUP * chunk),
                lambda i: (jnp.minimum(i, steps - 1), 0, 0, 0),
                memory_space=pltpu.SMEM,
            ),
            pl.BlockSpec(
                table.shape, lambda i: (0, 0, 0), pipeline_mode=pl.Buffered(1)
            ),
            pl.BlockSpec(
                (1, GROUP * width, width), lambda i: (jnp.maximum(i - 1, 0), 0, 0)
            ),
        ],
        out_specs=pl.BlockSpec((targets, width), lambda i: (0, 0)),
        scratch_shapes=[pltpu.VMEM((GROUP // 2, targets, 2 * width), jnp.float32)],
        compiler_params=pltpu.CompilerParams(
            vmem_limit_bytes=48 * 1024 * 1024, dimension_semantics=("arbitrary",)
        ),
    )(jnp.arange(BATCH, dtype=jnp.int32), index, table, weights)


def per_device(fine_multipole, coarse_multipole, kernels, send_list, fine_source, coarse_source):
    width = fine_multipole.shape[0]
    reach_each = send_list.shape[1] // 2
    ghost_slots = send_list.shape[2]
    near_steps = [
        j - reach_each if j < reach_each else j - reach_each + 1 for j in range(2 * reach_each)
    ]
    own = jnp.transpose(fine_multipole)
    sub = lax.axis_index("sub")
    mine = lax.dynamic_slice_in_dim(send_list[0], sub * reach_each, reach_each, 0)
    outgoing = jnp.take(own, mine.reshape(-1), axis=0, mode="clip").reshape(
        reach_each, ghost_slots, width
    )
    outgoing = side_by_side(outgoing)
    ranges, subs = lax.axis_size("morton"), lax.axis_size("sub")
    arrivals = []
    for k in range(reach_each):
        route = [
            (q * subs + s, (q - near_steps[s * reach_each + k]) * subs + s)
            for q in range(ranges)
            for s in range(subs)
            if 0 <= q - near_steps[s * reach_each + k] < ranges
        ]
        arrivals.append(lax.ppermute(outgoing[k], ("morton", "sub"), route))
    here = jnp.stack(arrivals)
    there = lax.ppermute(here, "sub", [(0, 1), (1, 0)])
    ghosts = jnp.concatenate(
        [jnp.where(sub == 0, here, there), jnp.where(sub == 0, there, here)], axis=0
    )
    ghosts = one_below_other(ghosts).reshape(-1, width)
    coarse = lax.all_gather(
        side_by_side(jnp.transpose(coarse_multipole)[None]), ("morton", "sub"), axis=0, tiled=True
    )
    coarse = one_below_other(coarse).reshape(-1, width)
    blank = jnp.zeros((BLANK, width), jnp.bfloat16)
    rows = jnp.concatenate([own, ghosts, blank, coarse, blank], axis=0)
    rows = rows.astype(jnp.float32)
    table = jnp.concatenate([rows, rows], axis=1)[:, None, :]
    no_source = own.shape[0] + 2 * reach_each * ghost_slots
    fine_half = fine_source.shape[1] // 2
    coarse_half = coarse_source.shape[1] // 2
    coarse_index = coarse_source + (no_source + BLANK)
    lists = jnp.concatenate(
        [
            fine_source[:, :fine_half],
            coarse_index[:, :coarse_half],
            fine_source[:, fine_half:],
            coarse_index[:, coarse_half:],
        ],
        axis=1,
    )
    extra = -lists.shape[0] % GROUP
    lists = jnp.pad(lists, ((0, extra), (0, 0)), constant_values=no_source)
    part = translate(kernels, table, lists)
    local = lax.psum_scatter(part, "sub", scatter_dimension=0, tiled=True)
    local = jnp.transpose(local)
    return local[:, :fine_half], 0.5 * local[:, fine_half:]


def solution(mesh):
    placed = (
        P(None, "morton"),
        P(None, ("morton", "sub")),
        P("sub", None, None),
        P("morton", None, None),
        P("sub", "morton"),
        P("sub", "morton"),
    )
    return jax.shard_map(
        per_device,
        mesh=mesh,
        in_specs=placed,
        out_specs=(P(None, ("morton", "sub")), P(None, ("morton", "sub"))),
        check_vma=False,
    )
```
